32 devices in a mesh: node: 8 (over z, y), feat: 4 (over x, core).
Axes of the slice: x: 2, y: 2, z: 4, core: 2. Of those that a mesh axis runs over, the one named last changes fastest.
Arguments:
- features: bfloat16 [32768, 256], P(('node', 'feat')), may hold values from -6 to 6
- weight: bfloat16 [256, 256], replicated, may hold values from -1.5 to 1.5
- grad_out: bfloat16 [32768, 256], P(('node', 'feat')), may hold values from -6 to 6
- local_rows: int32 [8, 4, 32], P('node', 'feat'), may hold values from 0 to 7
- local_cols: int32 [8, 4, 32], P('node', 'feat'), may hold values from 0 to 31
- local_values: bfloat16 [8, 4, 32, 128, 128], P('node', 'feat'), may hold values from 0 to 3, as said below
- remote_rows: int32 [8, 4, 3, 16], P('node', 'feat'), may hold values from 0 to 7
- remote_slots: int32 [8, 4, 3, 16], P('node', 'feat'), may hold values from 0 to 15
- remote_values: bfloat16 [8, 4, 3, 16, 128, 128], P('node', 'feat'), may hold values from 0 to 3, as said below
- send_blocks: int32 [8, 3, 16], P('node'), may hold values from 0 to 31, as said below
- tile_counts: int32 [8, 4, 4], P('node', 'feat'), may hold values from 1 to 32, as said below
Outputs:
- output: bfloat16 [32768, 256], P(('node', 'feat'))
- grad_features: bfloat16 [32768, 256], P(('node', 'feat'))
The draws below stay inside these ranges and needn't reach their ends.
Inputs may be any that keep to these rules, and one draw needn't show every extreme that they name: `tile_counts`: column 0 is at most 32 and every other column at most 16; each column reaches its bound on some device, and other devices hold all, a half or a quarter of it, at least 1. `send_blocks`: the 16 blocks of one part and round are distinct. `local_values`: each entry is zero or a positive edge weight. `remote_values`: each entry is zero or a positive edge weight.
All inputs are finite; a program needn't handle non-finite values.
Results may differ from the reference program's by a relative error of at most 0.0049.
Values may be sent and summed in bfloat16 or wider, within the bound.
A program may use at most 128 MiB of HBM per device.

```python
import jax
import jax.numpy as jnp
from jax import lax

F = 256
BLOCK = 128
BLOCKS_DEV = 8
ROUNDS = 3
BLOCKS_PART = 32
NEED = 16
LOCAL_CAP = 32
REMOTE_CAP = 16
PARTS_SIZE = 8
NODES = 32768
N_NODE = 8
N_FEAT = 4


def tile_draw(key, shape):
    key_mask, key_value = jax.random.split(key)
    kept_mask = jax.random.randint(key_mask, shape, 0, BLOCK) < 4
    weights = jnp.exp(jax.random.uniform(key_value, shape, jnp.float32, -0.7, 0.7))
    return jnp.where(kept_mask, weights, jnp.float32(0.0)).astype(jnp.bfloat16)


def draw_local_values(key, part):
    return tile_draw(key, (PARTS_SIZE, N_FEAT, LOCAL_CAP, BLOCK, BLOCK))


def draw_remote_values(key, part):
    return tile_draw(key, (PARTS_SIZE, N_FEAT, ROUNDS, REMOTE_CAP, BLOCK, BLOCK))


def pick_blocks(single_key):
    return jax.random.permutation(single_key, BLOCKS_PART)[:NEED]


def draw_send_blocks(key, part):
    all_keys = jax.random.split(key, PARTS_SIZE * ROUNDS)
    picked = jax.vmap(pick_blocks)(all_keys)
    return picked.reshape(PARTS_SIZE, ROUNDS, NEED).astype(jnp.int32)


def draw_tile_counts(key, part):
    key_shift, key_top = jax.random.split(key)
    device_count = PARTS_SIZE * N_FEAT
    shifts = jax.random.randint(key_shift, (device_count, ROUNDS + 1), 0, 3)
    limits = jnp.concatenate([jnp.full((1,), LOCAL_CAP, jnp.int32), jnp.full((ROUNDS,), REMOTE_CAP, jnp.int32)])
    divisor = jnp.left_shift(jnp.ones((device_count, ROUNDS + 1), jnp.int32), shifts)
    counts = jnp.maximum(limits[None, :] // divisor, 1)
    topmost = jax.random.randint(key_top, (ROUNDS + 1,), 0, device_count)
    device_ids = jnp.arange(device_count, dtype=jnp.int32)
    counts = jnp.where(device_ids[:, None] == topmost[None, :], limits[None, :], counts)
    return counts.reshape(PARTS_SIZE, N_FEAT, ROUNDS + 1).astype(jnp.int32)


def with_ends(values, rng, least, high):
    longest = values.shape.index(max(values.shape))
    spots = []
    for shift in (0, 1):
        where = [jax.random.randint(jax.random.fold_in(rng, axis), (), 0, length) for axis, length in enumerate(values.shape)]
        where[longest] = (where[longest] + shift) % values.shape[longest]
        spots.append(tuple(where))
    return values.at[spots[0]].set(least).at[spots[1]].set(high)


def level_of(stream_key, extent, pieces, smallest, top_value):
    def one(position, shards_of):
        steps = jax.random.uniform(jax.random.fold_in(jax.random.fold_in(stream_key, 6), position), (shards_of,), jnp.float32, smallest / len(pieces), top_value / len(pieces))
        return jnp.repeat(jnp.exp(steps), extent[position] // shards_of).reshape((-1,) + (1,) * (len(extent) - position - 1))

    gain = one(*pieces[0])
    for cut in pieces[1:]:
        gain = gain * one(*cut)
    return gain


def normal_values(own_key, shape, scale, limit, shards=(), kind=jnp.bfloat16):
    result = scale * jax.random.normal(own_key, shape, jnp.float32)
    if shards:
        result = result * level_of(own_key, shape, shards, -0.22, 0.18)
    return jnp.clip(result, -limit, limit).astype(kind)


def setup_inputs(seed: int = 0) -> dict:
    arg_keys = jax.random.split(jax.random.key(seed), 12)
    features = normal_values(arg_keys[0], (NODES, F), 1.0, 6.0, ((0, 32),))
    weight = normal_values(arg_keys[1], (F, F), (F // 16) ** -0.5, 1.5)
    grad_out = normal_values(arg_keys[2], (NODES, F), 1.0, 6.0, ((0, 32),))
    local_rows = with_ends(jax.random.randint(arg_keys[3], (PARTS_SIZE, N_FEAT, LOCAL_CAP), 0, BLOCKS_DEV), jax.random.fold_in(arg_keys[3], 1), 0, BLOCKS_DEV - 1).astype(jnp.int32)
    local_cols = with_ends(jax.random.randint(arg_keys[4], (PARTS_SIZE, N_FEAT, LOCAL_CAP), 0, BLOCKS_PART), jax.random.fold_in(arg_keys[4], 1), 0, BLOCKS_PART - 1).astype(jnp.int32)
    local_values = draw_local_values(jax.random.fold_in(arg_keys[11], 71), 0)
    remote_rows = with_ends(jax.random.randint(arg_keys[6], (PARTS_SIZE, N_FEAT, ROUNDS, REMOTE_CAP), 0, BLOCKS_DEV), jax.random.fold_in(arg_keys[6], 1), 0, BLOCKS_DEV - 1).astype(jnp.int32)
    remote_slots = with_ends(jax.random.randint(arg_keys[7], (PARTS_SIZE, N_FEAT, ROUNDS, REMOTE_CAP), 0, NEED), jax.random.fold_in(arg_keys[7], 1), 0, NEED - 1).astype(jnp.int32)
    remote_values = draw_remote_values(jax.random.fold_in(arg_keys[11], 71), 0)
    send_blocks = draw_send_blocks(jax.random.fold_in(arg_keys[11], 71), 0)
    tile_counts = draw_tile_counts(jax.random.fold_in(arg_keys[11], 71), 0)
    return dict(features=features, weight=weight, grad_out=grad_out, local_rows=local_rows, local_cols=local_cols, local_values=local_values, remote_rows=remote_rows, remote_slots=remote_slots, remote_values=remote_values, send_blocks=send_blocks, tile_counts=tile_counts)


def part_blocks(table, part_id):
    rows = BLOCKS_PART * BLOCK
    piece = lax.dynamic_slice_in_dim(table, (part_id * rows).astype(jnp.int32), rows, 0)
    return piece.reshape(BLOCKS_PART, BLOCK, F)


def spread(one_hot, values):
    return jnp.einsum('tb,tif->bif', one_hot, values, precision=lax.Precision.HIGHEST)


def block_hot(targets, live):
    block_ids = jnp.arange(BLOCKS_PART, dtype=jnp.int32)
    return ((targets[:, None] == block_ids[None, :]) & live[:, None]).astype(jnp.float32)


def round_bits():
    log_nodes = int(N_NODE).bit_length() - 1
    return [(round_no * log_nodes) // ROUNDS for round_no in range(ROUNDS)]


def reference(features, weight, grad_out, local_rows, local_cols, local_values, remote_rows, remote_slots, remote_values, send_blocks, tile_counts):
    bits = round_bits()
    part_ids = jnp.arange(PARTS_SIZE, dtype=jnp.int32)
    offsets = (jnp.arange(N_FEAT, dtype=jnp.int32) * BLOCKS_DEV)[:, None]
    local_slot = jnp.arange(LOCAL_CAP, dtype=jnp.int32)[None, :]
    remote_slot = jnp.arange(REMOTE_CAP, dtype=jnp.int32)[None, :]

    def forward(part_id):
        own = part_blocks(features, part_id).astype(jnp.float32)
        counts = tile_counts[part_id]
        dests = (local_rows[part_id] + offsets).reshape(-1)
        sources_ids = local_cols[part_id].reshape(-1)
        tile_vals = local_values[part_id].astype(jnp.float32).reshape(-1, BLOCK, BLOCK)
        live = (local_slot < counts[:, 0:1]).reshape(-1)
        one_hot = block_hot(dests, live)
        product = jnp.einsum('tij,tjf->tif', tile_vals, own[sources_ids], precision=lax.Precision.HIGHEST)
        totals = own + spread(one_hot, product)
        rowsum = jnp.einsum('tb,ti->bi', one_hot, jnp.sum(tile_vals, axis=-1), precision=lax.Precision.HIGHEST)
        for round_no, bit_no in enumerate(bits):
            partner = jnp.bitwise_xor(part_id, jnp.int32(1 << bit_no))
            source_ids = send_blocks[partner, round_no][remote_slots[part_id, :, round_no]].reshape(-1)
            sources = part_blocks(features, partner).astype(jnp.float32)[source_ids]
            rvals = remote_values[part_id, :, round_no].astype(jnp.float32).reshape(-1, BLOCK, BLOCK)
            rlive = (remote_slot < counts[:, round_no + 1:round_no + 2]).reshape(-1)
            rdests = (remote_rows[part_id, :, round_no] + offsets).reshape(-1)
            rhot = block_hot(rdests, rlive)
            rprod = jnp.einsum('tij,tjf->tif', rvals, sources, precision=lax.Precision.HIGHEST)
            totals = totals + spread(rhot, rprod)
            rowsum = rowsum + jnp.einsum('tb,ti->bi', rhot, jnp.sum(rvals, axis=-1), precision=lax.Precision.HIGHEST)
        degree = 1.0 + rowsum
        hidden = (totals / degree[:, :, None]).astype(jnp.bfloat16)
        return hidden, degree

    hidden, degree = lax.map(forward, part_ids)
    hidden = hidden.reshape(NODES, F)
    degree = degree.reshape(NODES)
    output = jnp.dot(hidden, weight, preferred_element_type=jnp.float32).astype(jnp.bfloat16)
    grad_dense = jnp.dot(grad_out, weight.T, preferred_element_type=jnp.float32)
    grad_hidden = (grad_dense / degree[:, None]).astype(jnp.bfloat16)

    def backward(part_id):
        own = part_blocks(grad_hidden, part_id).astype(jnp.float32)
        counts = tile_counts[part_id]
        dests = (local_rows[part_id] + offsets).reshape(-1)
        sources_ids = local_cols[part_id].reshape(-1)
        tile_vals = local_values[part_id].astype(jnp.float32).reshape(-1, BLOCK, BLOCK)
        live = (local_slot < counts[:, 0:1]).reshape(-1)
        back = jnp.einsum('tij,tif->tjf', tile_vals, own[dests], precision=lax.Precision.HIGHEST)
        grad_sum = own + spread(block_hot(sources_ids, live), back)
        for round_no, bit_no in enumerate(bits):
            partner = jnp.bitwise_xor(part_id, jnp.int32(1 << bit_no))
            peer_grad = part_blocks(grad_hidden, partner).astype(jnp.float32)
            pvals = remote_values[partner, :, round_no].astype(jnp.float32).reshape(-1, BLOCK, BLOCK)
            plive = (remote_slot < tile_counts[partner, :, round_no + 1:round_no + 2]).reshape(-1)
            pdests = (remote_rows[partner, :, round_no] + offsets).reshape(-1)
            pback = jnp.einsum('tij,tif->tjf', pvals, peer_grad[pdests], precision=lax.Precision.HIGHEST)
            targets = send_blocks[part_id, round_no][remote_slots[partner, :, round_no].reshape(-1)]
            grad_sum = grad_sum + spread(block_hot(targets, plive), pback)
        return grad_sum.astype(jnp.bfloat16)

    grad_features = lax.map(backward, part_ids).reshape(NODES, F)
    return output, grad_features
```

```python
import functools

import jax
import jax.numpy as jnp
from jax import lax
from jax.experimental import pallas as pl
from jax.experimental.pallas import tpu as pltpu
from jax.sharding import PartitionSpec as P

F32 = jnp.float32
BF16 = jnp.bfloat16
VMEM_LIMIT = 56 * 2**20
GROUP = 8


def dot(a, b):
    return jnp.dot(a, b, preferred_element_type=F32)


def dot_tn(a, b):
    return lax.dot_general(a, b, (((0,), (0,)), ((), ())), preferred_element_type=F32)


def dot_nt(a, b):
    return lax.dot_general(a, b, (((1,), (1,)), ((), ())), preferred_element_type=F32)


def grouped(slots, step):
    group = min(GROUP, slots)
    assert slots % group == 0

    @pl.loop(0, slots // group)
    def _(g):
        step([g * group + u for u in range(group)])


def backward_kernel(
    grad_out,
    weight,
    local_rows,
    local_cols,
    local_values,
    remote_rows,
    remote_slots,
    remote_values,
    send_blocks,
    counts,
    acc,
    parcel,
    grad_hidden,
    degree,
    place,
    parcel_sum,
    degree_sum,
):
    block = local_values.shape[-1]
    own = grad_out.shape[0] // block
    part = acc.shape[0] - 1
    rounds, need = send_blocks.shape[1:]
    feat = grad_out.shape[1]
    for r in range(rounds):

        @pl.loop(0, part)
        def _(b):
            place[r, b] = -1

        @pl.loop(0, need)
        def _(i):
            place[r, send_blocks[0, r, i]] = i

    ones = jnp.ones((block, block), BF16)
    degree_sum[...] = jnp.ones_like(degree_sum)
    acc[...] = jnp.zeros_like(acc)
    parcel_sum[...] = jnp.zeros_like(parcel_sum)

    def local_degree(ts):
        sums = [dot(local_values[0, 0, t], ones) for t in ts]
        for t, s in zip(ts, sums):
            to = jnp.where(t < counts[0, 0, 0], local_rows[0, 0, t], own)
            degree_sum[to] += s

    grouped(local_values.shape[2], local_degree)
    for r in range(rounds):

        def remote_degree(ts):
            sums = [dot(remote_values[0, 0, r, t], ones) for t in ts]
            for t, s in zip(ts, sums):
                to = jnp.where(t < counts[0, 0, r + 1], remote_rows[0, 0, r, t], own)
                degree_sum[to] += s

        grouped(remote_values.shape[3], remote_degree)

    for d in range(own):
        rows = pl.ds(d * block, block)
        deg = degree_sum[d]
        degree[d] = deg
        dense = dot_nt(grad_out[rows, :], weight[...])
        wide = jnp.concatenate([deg] * (feat // block), axis=1)
        grad_hidden[d] = (dense / wide).astype(BF16)

    for r in range(rounds):

        def remote_back(ts):
            prods = [
                dot_tn(remote_values[0, 0, r, t], grad_hidden[remote_rows[0, 0, r, t]])
                for t in ts
            ]
            for t, p in zip(ts, prods):
                to = jnp.where(t < counts[0, 0, r + 1], remote_slots[0, 0, r, t], need)
                parcel_sum[r, to] += p

        grouped(remote_values.shape[3], remote_back)
        parcel[r] = parcel_sum[r, :need].astype(BF16)

    def local_back(ts):
        prods = [dot_tn(local_values[0, 0, t], grad_hidden[local_rows[0, 0, t]]) for t in ts]
        for t, p in zip(ts, prods):
            to = jnp.where(t < counts[0, 0, 0], local_cols[0, 0, t], part)
            acc[to] += p

    grouped(local_values.shape[2], local_back)


def forward_kernel(
    features,
    weight,
    local_rows,
    local_cols,
    local_values,
    remote_rows,
    remote_slots,
    remote_values,
    counts,
    degree,
    part_feats,
    arrived,
    output,
    totals,
):
    block = local_values.shape[-1]
    own = features.shape[0] // block
    rounds = remote_values.shape[2]
    feat = features.shape[1]
    for d in range(own):
        totals[d] = features[pl.ds(d * block, block), :].astype(F32)
    totals[own] = jnp.zeros_like(totals[own])

    def local_step(ts):
        prods = [dot(local_values[0, 0, t], part_feats[local_cols[0, 0, t]]) for t in ts]
        for t, p in zip(ts, prods):
            to = jnp.where(t < counts[0, 0, 0], local_rows[0, 0, t], own)
            totals[to] += p

    grouped(local_values.shape[2], local_step)
    for r in range(rounds):

        def remote_step(ts):
            prods = [
                dot(remote_values[0, 0, r, t], arrived[r, remote_slots[0, 0, r, t]]) for t in ts
            ]
            for t, p in zip(ts, prods):
                to = jnp.where(t < counts[0, 0, r + 1], remote_rows[0, 0, r, t], own)
                totals[to] += p

        grouped(remote_values.shape[3], remote_step)
    for d in range(own):
        wide = jnp.concatenate([degree[d]] * (feat // block), axis=1)
        hidden = (totals[d] / wide).astype(BF16)
        output[pl.ds(d * block, block), :] = dot(hidden, weight[...]).astype(BF16)


def exchange_kernel(
    bits,
    feat_size,
    features,
    send_blocks,
    place,
    acc,
    parcel,
    grad_hidden,
    part_feats,
    arrived,
    grad_features,
    send_buf,
    mate_parcel,
    parcel_out,
    returned,
    pair_out,
    pair_in,
    kept,
    cross_out,
    cross_in,
    feat_send,
    feat_recv,
    node_send,
    node_recv,
    pass_send,
    pass_recv,
    parcel_send,
    parcel_recv,
    back_send,
    back_recv,
    red_send,
    red_recv,
):
    rounds = len(bits)
    own, block, _ = grad_hidden.shape
    need = parcel.shape[1]
    half = need // 2
    node, f = lax.axis_index("node"), lax.axis_index("feat")
    h = lax.rem(f, 2)
    mate_h = 1 - h
    mate = f + 1 - 2 * h
    opp = lax.rem(f + 2, feat_size)
    partners = [node + (1 << b) * (1 - 2 * lax.rem(node // (1 << b), 2)) for b in bits]
    to_mate, to_opp = (node, mate), (node, opp)
    to_node = [(p, f) for p in partners]

    def remote(src, dst, send_sem, recv_sem, to):
        copy = pltpu.make_async_remote_copy(
            src_ref=src,
            dst_ref=dst,
            send_sem=send_sem,
            recv_sem=recv_sem,
            device_id=to,
            device_id_type=pl.DeviceIdType.MESH,
        )
        return copy

    barrier = pltpu.get_barrier_semaphore()
    for to in (to_mate, to_opp, *to_node):
        pl.semaphore_signal(barrier, inc=1, device_id=to, device_id_type=pl.DeviceIdType.MESH)
    pl.semaphore_wait(barrier, 2 + rounds)

    mine = part_feats.at[pl.ds(f * own, own)]
    for b in range(own):
        part_feats[f * own + b] = features[pl.ds(b * block, block), :]
    cross = remote(mine, mine, feat_send.at[0], feat_recv.at[0], to_opp)
    cross.start()
    pair = remote(mine, mine, feat_send.at[1], feat_recv.at[1], to_mate)
    pair.start()
    order = list(range(rounds))[::-1]
    swaps = [None] * rounds
    for r in order:
        swaps[r] = remote(
            parcel.at[r, pl.ds(mate_h * half, half)],
            mate_parcel.at[r],
            parcel_send.at[r],
            parcel_recv.at[r],
            to_mate,
        )
        swaps[r].start()
    backs = [None] * rounds
    for r in order:
        swaps[r].wait()

        @pl.loop(0, half)
        def _(i):
            total = parcel[r, h * half + i].astype(F32) + mate_parcel[r, i].astype(F32)
            parcel_out[r, i] = total.astype(BF16)

        backs[r] = remote(
            parcel_out.at[r], returned.at[r], back_send.at[r], back_recv.at[r], to_node[r]
        )
        backs[r].start()

    cross.wait()
    theirs = part_feats.at[pl.ds(opp * own, own)]
    relay = remote(theirs, theirs, feat_send.at[2], feat_recv.at[2], to_mate)
    relay.start()
    pair.wait()
    relay.wait()
    outs = [None] * rounds
    for r in order:

        @pl.loop(0, half)
        def _(i):
            send_buf[r, i] = part_feats[send_blocks[0, r, h * half + i]]

        outs[r] = remote(
            send_buf.at[r],
            arrived.at[r, pl.ds(h * half, half)],
            node_send.at[r],
            node_recv.at[r],
            to_node[r],
        )
        outs[r].start()

    for r in order:
        backs[r].wait()

    def gathered_sum(b):
        total = acc[b]
        for r in range(rounds):
            at = place[r, b] - h * half
            there = jnp.logical_and(at >= 0, at < half)
            found = returned[r, jnp.clip(at, 0, half - 1)].astype(F32)
            total = total + jnp.where(there, found, 0.0)
        return total

    for o in range(feat_size // 2):

        @pl.loop(0, own)
        def _(j):
            pair_out[o, j] = gathered_sum((2 * o + mate_h) * own + j).astype(BF16)

    pair_red = remote(pair_out, pair_in, red_send.at[0], red_recv.at[0], to_mate)
    pair_red.start()
    for o in range(feat_size // 2):

        @pl.loop(0, own)
        def _(j):
            kept[o, j] = gathered_sum((2 * o + h) * own + j)

    pair_red.wait()

    @pl.loop(0, own)
    def _(j):
        o = opp // 2
        cross_out[j] = (kept[o, j] + pair_in[o, j].astype(F32)).astype(BF16)

    cross_red = remote(cross_out, cross_in, red_send.at[1], red_recv.at[1], to_opp)
    cross_red.start()
    passes = [None] * rounds
    for r in order[::-1]:
        outs[r].wait()
        piece = arrived.at[r, pl.ds(h * half, half)]
        passes[r] = remote(piece, piece, pass_send.at[r], pass_recv.at[r], to_mate)
        passes[r].start()
    cross_red.wait()
    for j in range(own):
        o = f // 2
        total = kept[o, j] + pair_in[o, j].astype(F32)
        total = total + cross_in[j].astype(F32) + grad_hidden[j].astype(F32)
        grad_features[pl.ds(j * block, block), :] = total.astype(BF16)
    for r in range(rounds):
        passes[r].wait()


def body(
    features,
    weight,
    grad_out,
    local_rows,
    local_cols,
    local_values,
    remote_rows,
    remote_slots,
    remote_values,
    send_blocks,
    tile_counts,
):
    rows_dev, feat = features.shape
    block = local_values.shape[-1]
    own = rows_dev // block
    rounds, need = send_blocks.shape[1:]
    feat_size = lax.axis_size("feat")
    part = own * feat_size
    log_nodes = lax.axis_size("node").bit_length() - 1
    bits = [r * log_nodes // rounds for r in range(rounds)]
    half = need // 2
    assert feat_size == 4
    vmem = pl.BlockSpec(memory_space=pltpu.VMEM)
    smem = pl.BlockSpec(memory_space=pltpu.SMEM)
    tile_flops = 2 * block * block * feat * (local_values.shape[2] + rounds * need)
    acc, parcel, grad_hidden, degree, place = pl.pallas_call(
        backward_kernel,
        out_shape=(
            jax.ShapeDtypeStruct((part + 1, block, feat), F32),
            jax.ShapeDtypeStruct((rounds, need, block, feat), BF16),
            jax.ShapeDtypeStruct((own, block, feat), BF16),
            jax.ShapeDtypeStruct((own, block, block), F32),
            jax.ShapeDtypeStruct((rounds, part), jnp.int32),
        ),
        in_specs=[vmem, vmem, smem, smem, vmem, smem, smem, vmem, smem, smem],
        out_specs=(vmem, vmem, vmem, vmem, smem),
        scratch_shapes=[
            pltpu.VMEM((rounds, need + 1, block, feat), F32),
            pltpu.VMEM((own + 1, block, block), F32),
        ],
        compiler_params=pltpu.CompilerParams(vmem_limit_bytes=VMEM_LIMIT),
        cost_estimate=pl.CostEstimate(
            flops=2 * tile_flops, bytes_accessed=12 * 2**20, transcendentals=0
        ),
        name="backward_products",
    )(
        grad_out,
        weight,
        local_rows,
        local_cols,
        local_values,
        remote_rows,
        remote_slots,
        remote_values,
        send_blocks,
        tile_counts,
    )
    dma = pltpu.SemaphoreType.DMA
    part_feats, arrived, grad_features = pl.pallas_call(
        functools.partial(exchange_kernel, bits, feat_size),
        out_shape=(
            jax.ShapeDtypeStruct((part, block, feat), BF16),
            jax.ShapeDtypeStruct((rounds, need, block, feat), BF16),
            jax.ShapeDtypeStruct((rows_dev, feat), BF16),
        ),
        in_specs=[vmem, smem, smem, vmem, vmem, vmem],
        out_specs=(vmem, vmem, vmem),
        scratch_shapes=[
            pltpu.VMEM((rounds, half, block, feat), BF16),
            pltpu.VMEM((rounds, half, block, feat), BF16),
            pltpu.VMEM((rounds, half, block, feat), BF16),
            pltpu.VMEM((rounds, half, block, feat), BF16),
            pltpu.VMEM((feat_size // 2, own, block, feat), BF16),
            pltpu.VMEM((feat_size // 2, own, block, feat), BF16),
            pltpu.VMEM((feat_size // 2, own, block, feat), F32),
            pltpu.VMEM((own, block, feat), BF16),
            pltpu.VMEM((own, block, feat), BF16),
            dma((3,)),
            dma((3,)),
            dma((rounds,)),
            dma((rounds,)),
            dma((rounds,)),
            dma((rounds,)),
            dma((rounds,)),
            dma((rounds,)),
            dma((rounds,)),
            dma((rounds,)),
            dma((2,)),
            dma((2,)),
        ],
        compiler_params=pltpu.CompilerParams(
            vmem_limit_bytes=VMEM_LIMIT, collective_id=0, has_side_effects=True
        ),
        cost_estimate=pl.CostEstimate(flops=0, bytes_accessed=20 * 2**20, transcendentals=0),
        name="exchange",
    )(features, send_blocks, place, acc, parcel, grad_hidden)
    output = pl.pallas_call(
        forward_kernel,
        out_shape=jax.ShapeDtypeStruct((rows_dev, feat), BF16),
        in_specs=[vmem, vmem, smem, smem, vmem, smem, smem, vmem, smem, vmem, vmem, vmem],
        out_specs=vmem,
        scratch_shapes=[pltpu.VMEM((own + 1, block, feat), F32)],
        compiler_params=pltpu.CompilerParams(vmem_limit_bytes=VMEM_LIMIT),
        cost_estimate=pl.CostEstimate(
            flops=tile_flops, bytes_accessed=10 * 2**20, transcendentals=0
        ),
        name="forward_products",
    )(
        features,
        weight,
        local_rows,
        local_cols,
        local_values,
        remote_rows,
        remote_slots,
        remote_values,
        tile_counts,
        degree,
        part_feats,
        arrived,
    )
    return (output, grad_features)


def solution(mesh):
    in_specs = (
        P(("node", "feat"), None),
        P(),
        P(("node", "feat"), None),
        P("node", "feat", None),
        P("node", "feat", None),
        P("node", "feat", None, None, None),
        P("node", "feat", None, None),
        P("node", "feat", None, None),
        P("node", "feat", None, None, None, None),
        P("node", None, None),
        P("node", "feat", None),
    )
    out_specs = (P(("node", "feat"), None), P(("node", "feat"), None))
    return jax.shard_map(body, mesh=mesh, in_specs=in_specs, out_specs=out_specs, check_vma=False)
```

```python
import functools

import jax
import jax.numpy as jnp
from jax import lax
from jax.experimental import pallas as pl
from jax.experimental.pallas import tpu as pltpu
from jax.sharding import PartitionSpec as P

F32 = jnp.float32
BF16 = jnp.bfloat16
VMEM_LIMIT = 56 * 2**20
GROUP = 8


def dot(a, b):
    return jnp.dot(a, b, preferred_element_type=F32)


def dot_tn(a, b):
    return lax.dot_general(a, b, (((0,), (0,)), ((), ())), preferred_element_type=F32)


def dot_nt(a, b):
    return lax.dot_general(a, b, (((1,), (1,)), ((), ())), preferred_element_type=F32)


def grouped(slots, step):
    group = min(GROUP, slots)
    assert slots % group == 0

    @pl.loop(0, slots // group)
    def _(g):
        step([g * group + u for u in range(group)])


class Layout:
    def __init__(self, slots, rounds, cap, need, own, part):
        self.slots, self.rounds, self.cap, self.need = slots, rounds, cap, need
        self.own, self.part = own, part
        sizes = (slots, slots, rounds * cap, rounds * cap, rounds * need, rounds + 1)
        starts = [sum(sizes[:i]) for i in range(len(sizes) + 1)]
        self.rows, self.cols, self.rrows, self.rslots, self.send, self.counts, _ = starts
        tiles = slots + rounds * cap
        sizes = (tiles, own, slots, part, rounds * cap, rounds * need, rounds * part)
        starts = [sum(sizes[:i]) for i in range(len(sizes) + 1)]
        self.prev_f, self.last_f, self.prev_l, self.last_l = starts[:4]
        self.prev_r, self.last_r, self.place, self.plan_size = starts[4:]
        self.tiles = tiles


def plan_kernel(
    lay, meta, grad_out, weight, local_values, remote_values, plan, grad_hidden, degree, degree_sum
):
    block = local_values.shape[-1]
    feat = grad_out.shape[1]

    @pl.loop(0, lay.plan_size)
    def _(i):
        plan[i] = -1

    @pl.loop(0, lay.slots)
    def _(t):
        @pl.when(t < meta[lay.counts])
        def _():
            d, c = meta[lay.rows + t], meta[lay.cols + t]
            plan[lay.prev_f + t] = plan[lay.last_f + d]
            plan[lay.last_f + d] = t
            plan[lay.prev_l + t] = plan[lay.last_l + c]
            plan[lay.last_l + c] = t

    for r in range(lay.rounds):

        @pl.loop(0, lay.cap)
        def _(t):
            at = r * lay.cap + t

            @pl.when(t < meta[lay.counts + r + 1])
            def _():
                d, c = meta[lay.rrows + at], meta[lay.rslots + at]
                plan[lay.prev_f + lay.slots + at] = plan[lay.last_f + d]
                plan[lay.last_f + d] = lay.slots + at
                plan[lay.prev_r + at] = plan[lay.last_r + r * lay.need + c]
                plan[lay.last_r + r * lay.need + c] = at

        @pl.loop(0, lay.need)
        def _(i):
            plan[lay.place + r * lay.part + meta[lay.send + r * lay.need + i]] = i

    ones = jnp.ones((block, block), BF16)
    degree_sum[...] = jnp.ones_like(degree_sum)

    def local_degree(ts):
        sums = [dot(local_values[0, 0, t], ones) for t in ts]
        for t, s in zip(ts, sums):
            to = jnp.where(t < meta[lay.counts], meta[lay.rows + t], lay.own)
            degree_sum[to] += s

    grouped(lay.slots, local_degree)
    for r in range(lay.rounds):

        def remote_degree(ts):
            sums = [dot(remote_values[0, 0, r, t], ones) for t in ts]
            for t, s in zip(ts, sums):
                live = t < meta[lay.counts + r + 1]
                to = jnp.where(live, meta[lay.rrows + r * lay.cap + t], lay.own)
                degree_sum[to] += s

        grouped(lay.cap, remote_degree)

    for d in range(lay.own):
        deg = degree_sum[d]
        degree[d] = deg
        dense = dot_nt(grad_out[pl.ds(d * block, block), :], weight[...])
        wide = jnp.concatenate([deg] * (feat // block), axis=1)
        grad_hidden[d] = (dense / wide).astype(BF16)


def exchange_kernel(
    lay,
    bits,
    feat_size,
    meta,
    plan,
    features,
    weight,
    local_values,
    remote_values,
    grad_hidden,
    degree,
    output,
    grad_features,
    part_feats,
    send_buf,
    mate_out,
    mate_parcel,
    parcel_out,
    returned,
    pair_out,
    pair_in,
    kept,
    cross_out,
    cross_in,
    sums_r,
    sums_l,
    sums_f,
    feat_send,
    feat_recv,
    node_send,
    node_recv,
    pass_send,
    pass_recv,
    parcel_send,
    parcel_recv,
    back_send,
    back_recv,
    red_send,
    red_recv,
    *arrived,
):
    rounds = len(bits)
    own, block, feat = grad_hidden.shape
    need, half = lay.need, lay.need // 2
    node, f = lax.axis_index("node"), lax.axis_index("feat")
    h = lax.rem(f, 2)
    mate_h = 1 - h
    mate = f + 1 - 2 * h
    opp = lax.rem(f + 2, feat_size)
    partners = [node + (1 << b) * (1 - 2 * lax.rem(node // (1 << b), 2)) for b in bits]
    to_mate, to_opp = (node, mate), (node, opp)
    to_node = [(p, f) for p in partners]

    def remote(src, dst, send_sem, recv_sem, to):
        return pltpu.make_async_remote_copy(
            src_ref=src,
            dst_ref=dst,
            send_sem=send_sem,
            recv_sem=recv_sem,
            device_id=to,
            device_id_type=pl.DeviceIdType.MESH,
        )

    barrier = pltpu.get_barrier_semaphore()
    for to in (to_mate, to_opp, *to_node):
        pl.semaphore_signal(barrier, inc=1, device_id=to, device_id_type=pl.DeviceIdType.MESH)
    pl.semaphore_wait(barrier, 2 + rounds)

    mine = part_feats.at[pl.ds(f * own, own)]
    for b in range(own):
        part_feats[f * own + b] = features[pl.ds(b * block, block), :]
    cross = remote(mine, mine, feat_send.at[0], feat_recv.at[0], to_opp)
    cross.start()
    pair = remote(mine, mine, feat_send.at[1], feat_recv.at[1], to_mate)
    pair.start()
    order = list(range(rounds))[::-1]

    def picked(sums, at):
        return jnp.where(at >= 0, sums[jnp.maximum(at, 0)], 0.0)

    def chain(sums, base, ts, prods, prev):
        for t, p in zip(ts, prods):
            sums[base + t] = p + picked(sums, plan[prev + t])

    def back_products(r):
        def step(ts):
            prods = [
                dot_tn(remote_values[0, 0, r, t], grad_hidden[meta[lay.rrows + r * lay.cap + t]])
                for t in ts
            ]
            chain(sums_r, r * lay.cap, ts, prods, lay.prev_r + r * lay.cap)

        grouped(lay.cap, step)

    def parcel(r, s):
        return picked(sums_r, plan[lay.last_r + r * need + s])

    swaps, backs = [None] * rounds, [None] * rounds

    def send_back(r):
        swaps[r].wait()

        @pl.loop(0, half)
        def _(i):
            total = parcel(r, h * half + i) + mate_parcel[r, i].astype(F32)
            parcel_out[r, i] = total.astype(BF16)

        backs[r] = remote(
            parcel_out.at[r], returned.at[r], back_send.at[r], back_recv.at[r], to_node[r]
        )
        backs[r].start()

    for k, r in enumerate(order):
        back_products(r)

        @pl.loop(0, half)
        def _(i):
            mate_out[r, i] = parcel(r, mate_h * half + i).astype(BF16)

        swaps[r] = remote(
            mate_out.at[r], mate_parcel.at[r], parcel_send.at[r], parcel_recv.at[r], to_mate
        )
        swaps[r].start()
        if k:
            send_back(order[k - 1])
    send_back(order[-1])

    cross.wait()
    theirs = part_feats.at[pl.ds(opp * own, own)]
    relay = remote(theirs, theirs, feat_send.at[2], feat_recv.at[2], to_mate)
    relay.start()
    pair.wait()
    relay.wait()
    outs = [None] * rounds
    for r in order:

        @pl.loop(0, half)
        def _(i):
            send_buf[r, i] = part_feats[meta[lay.send + r * need + h * half + i]]

        outs[r] = remote(
            send_buf.at[r],
            arrived[r].at[pl.ds(h * half, half)],
            node_send.at[r],
            node_recv.at[r],
            to_node[r],
        )
        outs[r].start()

    def local_back(ts):
        prods = [dot_tn(local_values[0, 0, t], grad_hidden[meta[lay.rows + t]]) for t in ts]
        chain(sums_l, 0, ts, prods, lay.prev_l)

    grouped(lay.slots, local_back)

    def local_forward(ts):
        prods = [dot(local_values[0, 0, t], part_feats[meta[lay.cols + t]]) for t in ts]
        chain(sums_f, 0, ts, prods, lay.prev_f)

    grouped(lay.slots, local_forward)

    for r in order[::-1]:
        backs[r].wait()

    def gathered_sum(b):
        total = picked(sums_l, plan[lay.last_l + b])
        for r in range(rounds):
            at = plan[lay.place + r * lay.part + b] - h * half
            there = jnp.logical_and(at >= 0, at < half)
            found = returned[r, jnp.clip(at, 0, half - 1)].astype(F32)
            total = total + jnp.where(there, found, 0.0)
        return total

    for o in range(feat_size // 2):

        @pl.loop(0, own)
        def _(j):
            pair_out[o, j] = gathered_sum((2 * o + mate_h) * own + j).astype(BF16)

    pair_red = remote(pair_out, pair_in, red_send.at[0], red_recv.at[0], to_mate)
    pair_red.start()
    for o in range(feat_size // 2):

        @pl.loop(0, own)
        def _(j):
            kept[o, j] = gathered_sum((2 * o + h) * own + j)

    pair_red.wait()

    @pl.loop(0, own)
    def _(j):
        o = opp // 2
        cross_out[j] = (kept[o, j] + pair_in[o, j].astype(F32)).astype(BF16)

    cross_red = remote(cross_out, cross_in, red_send.at[1], red_recv.at[1], to_opp)
    cross_red.start()
    passes = [None] * rounds

    def pass_on(r):
        outs[r].wait()
        piece = arrived[r].at[pl.ds(h * half, half)]
        passes[r] = remote(piece, piece, pass_send.at[r], pass_recv.at[r], to_mate)
        passes[r].start()

    def forward_products(r):
        passes[r].wait()

        def step(ts):
            prods = [
                dot(
                    remote_values[0, 0, r, t],
                    arrived[r][meta[lay.rslots + r * lay.cap + t]],
                )
                for t in ts
            ]
            base = lay.slots + r * lay.cap
            chain(sums_f, base, ts, prods, lay.prev_f + base)

        grouped(lay.cap, step)

    for r in range(rounds):
        pass_on(r)
        if r:
            forward_products(r - 1)
        if r == rounds - 2:
            cross_red.wait()
            for j in range(own):
                o = f // 2
                total = kept[o, j] + pair_in[o, j].astype(F32)
                total = total + cross_in[j].astype(F32) + grad_hidden[j].astype(F32)
                grad_features[pl.ds(j * block, block), :] = total.astype(BF16)
    forward_products(rounds - 1)
    for d in range(own):
        rows = pl.ds(d * block, block)
        total = features[rows, :].astype(F32) + picked(sums_f, plan[lay.last_f + d])
        wide = jnp.concatenate([degree[d]] * (feat // block), axis=1)
        hidden = (total / wide).astype(BF16)
        output[rows, :] = dot(hidden, weight[...]).astype(BF16)


def body(
    features,
    weight,
    grad_out,
    local_rows,
    local_cols,
    local_values,
    remote_rows,
    remote_slots,
    remote_values,
    send_blocks,
    tile_counts,
):
    rows_dev, feat = features.shape
    block = local_values.shape[-1]
    own = rows_dev // block
    rounds, need = send_blocks.shape[1:]
    feat_size = lax.axis_size("feat")
    part = own * feat_size
    log_nodes = lax.axis_size("node").bit_length() - 1
    bits = [r * log_nodes // rounds for r in range(rounds)]
    half = need // 2
    assert feat_size == 4
    vmem = pl.BlockSpec(memory_space=pltpu.VMEM)
    smem = pl.BlockSpec(memory_space=pltpu.SMEM)
    slots, cap = local_values.shape[2], remote_values.shape[3]
    lay = Layout(slots, rounds, cap, need, own, part)
    tile_flops = 2 * block * block * feat * lay.tiles
    ints = (local_rows, local_cols, remote_rows, remote_slots, send_blocks, tile_counts)
    meta = jnp.concatenate([a.reshape(-1) for a in ints])
    plan, grad_hidden, degree = pl.pallas_call(
        functools.partial(plan_kernel, lay),
        out_shape=(
            jax.ShapeDtypeStruct((lay.plan_size,), jnp.int32),
            jax.ShapeDtypeStruct((own, block, feat), BF16),
            jax.ShapeDtypeStruct((own, block, block), F32),
        ),
        in_specs=[smem, vmem, vmem, vmem, vmem],
        out_specs=(smem, vmem, vmem),
        scratch_shapes=[pltpu.VMEM((own + 1, block, block), F32)],
        compiler_params=pltpu.CompilerParams(vmem_limit_bytes=VMEM_LIMIT),
        cost_estimate=pl.CostEstimate(
            flops=tile_flops // 2, bytes_accessed=4 * 2**20, transcendentals=0
        ),
        name="plan",
    )(meta, grad_out, weight, local_values, remote_values)
    dma = pltpu.SemaphoreType.DMA
    halves = pltpu.VMEM((rounds, half, block, feat), BF16)
    pairs = (feat_size // 2, own, block, feat)
    output, grad_features = pl.pallas_call(
        functools.partial(exchange_kernel, lay, bits, feat_size),
        out_shape=(
            jax.ShapeDtypeStruct((rows_dev, feat), BF16),
            jax.ShapeDtypeStruct((rows_dev, feat), BF16),
        ),
        in_specs=[smem, smem, vmem, vmem, vmem, vmem, vmem, vmem],
        out_specs=(vmem, vmem),
        scratch_shapes=[
            pltpu.VMEM((part, block, feat), BF16),
            halves,
            halves,
            halves,
            halves,
            halves,
            pltpu.VMEM(pairs, BF16),
            pltpu.VMEM(pairs, BF16),
            pltpu.VMEM(pairs, F32),
            pltpu.VMEM((own, block, feat), BF16),
            pltpu.VMEM((own, block, feat), BF16),
            pltpu.VMEM((rounds * cap, block, feat), F32),
            pltpu.VMEM((slots, block, feat), F32),
            pltpu.VMEM((lay.tiles, block, feat), F32),
            dma((3,)),
            dma((3,)),
            *[dma((rounds,))] * 8,
            dma((2,)),
            dma((2,)),
            *[pltpu.VMEM((need, block, feat), BF16)] * rounds,
        ],
        compiler_params=pltpu.CompilerParams(
            vmem_limit_bytes=VMEM_LIMIT, collective_id=0, has_side_effects=True
        ),
        cost_estimate=pl.CostEstimate(
            flops=2 * tile_flops, bytes_accessed=8 * 2**20, transcendentals=0
        ),
        name="exchange",
    )(meta, plan, features, weight, local_values, remote_values, grad_hidden, degree)
    return (output, grad_features)


def solution(mesh):
    in_specs = (
        P(("node", "feat"), None),
        P(),
        P(("node", "feat"), None),
        P("node", "feat", None),
        P("node", "feat", None),
        P("node", "feat", None, None, None),
        P("node", "feat", None, None),
        P("node", "feat", None, None),
        P("node", "feat", None, None, None, None),
        P("node", None, None),
        P("node", "feat", None),
    )
    out_specs = (P(("node", "feat"), None), P(("node", "feat"), None))
    return jax.shard_map(body, mesh=mesh, in_specs=in_specs, out_specs=out_specs, check_vma=False)
```

```python
import functools

import jax
import jax.numpy as jnp
from jax import lax
from jax.experimental import pallas as pl
from jax.experimental.pallas import tpu as pltpu
from jax.sharding import PartitionSpec as P

F32 = jnp.float32
BF16 = jnp.bfloat16
VMEM_LIMIT = 56 * 2**20
GROUP = 8


def dot(a, b):
    return jnp.dot(a, b, preferred_element_type=F32)


def dot_tn(a, b):
    return lax.dot_general(a, b, (((0,), (0,)), ((), ())), preferred_element_type=F32)


def dot_nt(a, b):
    return lax.dot_general(a, b, (((1,), (1,)), ((), ())), preferred_element_type=F32)


def grouped(slots, step):
    group = min(GROUP, slots)
    assert slots % group == 0

    @pl.loop(0, slots // group)
    def _(g):
        step([g * group + u for u in range(group)])


class Layout:
    def __init__(self, slots, rounds, cap, need, own, part):
        self.slots, self.rounds, self.cap, self.need = slots, rounds, cap, need
        self.own, self.part = own, part
        sizes = (slots, slots, rounds * cap, rounds * cap, rounds * need, rounds + 1)
        starts = [sum(sizes[:i]) for i in range(len(sizes) + 1)]
        self.rows, self.cols, self.rrows, self.rslots, self.send, self.counts, _ = starts
        tiles = slots + rounds * cap
        sizes = (tiles, own, slots, part, rounds * cap, rounds * need, rounds * part)
        starts = [sum(sizes[:i]) for i in range(len(sizes) + 1)]
        self.prev_f, self.last_f, self.prev_l, self.last_l = starts[:4]
        self.prev_r, self.last_r, self.place, self.plan_size = starts[4:]
        self.tiles = tiles


def plan_kernel(
    lay, meta, grad_out, weight, local_values, remote_values, plan, grad_hidden, degree, degree_sum
):
    block = local_values.shape[-1]
    feat = grad_out.shape[1]

    @pl.loop(0, lay.plan_size)
    def _(i):
        plan[i] = -1

    @pl.loop(0, lay.slots)
    def _(t):
        @pl.when(t < meta[lay.counts])
        def _():
            d, c = meta[lay.rows + t], meta[lay.cols + t]
            plan[lay.prev_f + t] = plan[lay.last_f + d]
            plan[lay.last_f + d] = t
            plan[lay.prev_l + t] = plan[lay.last_l + c]
            plan[lay.last_l + c] = t

    for r in range(lay.rounds):

        @pl.loop(0, lay.cap)
        def _(t):
            at = r * lay.cap + t

            @pl.when(t < meta[lay.counts + r + 1])
            def _():
                d, c = meta[lay.rrows + at], meta[lay.rslots + at]
                plan[lay.prev_f + lay.slots + at] = plan[lay.last_f + d]
                plan[lay.last_f + d] = lay.slots + at
                plan[lay.prev_r + at] = plan[lay.last_r + r * lay.need + c]
                plan[lay.last_r + r * lay.need + c] = at

        @pl.loop(0, lay.need)
        def _(i):
            plan[lay.place + r * lay.part + meta[lay.send + r * lay.need + i]] = i

    ones = jnp.ones((block, block), BF16)
    degree_sum[...] = jnp.ones_like(degree_sum)

    def local_degree(ts):
        sums = [dot(local_values[0, 0, t], ones) for t in ts]
        for t, s in zip(ts, sums):
            to = jnp.where(t < meta[lay.counts], meta[lay.rows + t], lay.own)
            degree_sum[to] += s

    grouped(lay.slots, local_degree)
    for r in range(lay.rounds):

        def remote_degree(ts):
            sums = [dot(remote_values[0, 0, r, t], ones) for t in ts]
            for t, s in zip(ts, sums):
                live = t < meta[lay.counts + r + 1]
                to = jnp.where(live, meta[lay.rrows + r * lay.cap + t], lay.own)
                degree_sum[to] += s

        grouped(lay.cap, remote_degree)

    for d in range(lay.own):
        deg = degree_sum[d]
        degree[d] = deg
        dense = dot_nt(grad_out[pl.ds(d * block, block), :], weight[...])
        wide = jnp.concatenate([deg] * (feat // block), axis=1)
        grad_hidden[d] = (dense / wide).astype(BF16)


def exchange_kernel(
    lay,
    bits,
    feat_size,
    meta,
    plan,
    features,
    weight,
    local_values,
    remote_values,
    grad_hidden,
    degree,
    output,
    grad_features,
    part_feats,
    send_buf,
    mate_out,
    mate_parcel,
    parcel_out,
    returned,
    pair_out,
    pair_in,
    kept,
    cross_out,
    cross_in,
    sums_r,
    sums_l,
    sums_f,
    feat_send,
    feat_recv,
    node_send,
    node_recv,
    pass_send,
    pass_recv,
    parcel_send,
    parcel_recv,
    back_send,
    back_recv,
    red_send,
    red_recv,
    far_send,
    far_recv,
    far_in,
    *arrived,
):
    rounds = len(bits)
    own, block, feat = grad_hidden.shape
    need, half = lay.need, lay.need // 2
    node, f = lax.axis_index("node"), lax.axis_index("feat")
    h = lax.rem(f, 2)
    mate_h = 1 - h
    mate = f + 1 - 2 * h
    opp = lax.rem(f + 2, feat_size)
    partners = [node + (1 << b) * (1 - 2 * lax.rem(node // (1 << b), 2)) for b in bits]
    to_mate, to_opp = (node, mate), (node, opp)
    to_node = [(p, f) for p in partners]

    def remote(src, dst, send_sem, recv_sem, to):
        return pltpu.make_async_remote_copy(
            src_ref=src,
            dst_ref=dst,
            send_sem=send_sem,
            recv_sem=recv_sem,
            device_id=to,
            device_id_type=pl.DeviceIdType.MESH,
        )

    barrier = pltpu.get_barrier_semaphore()
    for to in (to_mate, to_opp, *to_node):
        pl.semaphore_signal(barrier, inc=1, device_id=to, device_id_type=pl.DeviceIdType.MESH)
    pl.semaphore_wait(barrier, 2 + rounds)

    mine = part_feats.at[pl.ds(f * own, own)]
    for b in range(own):
        part_feats[f * own + b] = features[pl.ds(b * block, block), :]
    cross = remote(mine, mine, feat_send.at[0], feat_recv.at[0], to_opp)
    cross.start()
    pair = remote(mine, mine, feat_send.at[1], feat_recv.at[1], to_mate)
    pair.start()
    order = list(range(rounds))[::-1]
    far, quarter = rounds - 1, half // 2

    def picked(sums, at):
        return jnp.where(at >= 0, sums[jnp.maximum(at, 0)], 0.0)

    def chain(sums, base, ts, prods, prev):
        for t, p in zip(ts, prods):
            sums[base + t] = p + picked(sums, plan[prev + t])

    def back_products(r):
        def step(ts):
            prods = [
                dot_tn(remote_values[0, 0, r, t], grad_hidden[meta[lay.rrows + r * lay.cap + t]])
                for t in ts
            ]
            chain(sums_r, r * lay.cap, ts, prods, lay.prev_r + r * lay.cap)

        grouped(lay.cap, step)

    def parcel(r, s):
        return picked(sums_r, plan[lay.last_r + r * need + s])

    swaps, backs = [None] * rounds, [None] * rounds

    def slot_of(r, side, i):
        if r == far:
            return (2 * (i // quarter) + side) * quarter + lax.rem(i, quarter)
        return side * half + i

    def swap_with_mate(r):
        back_products(r)

        @pl.loop(0, half)
        def _(i):
            mate_out[r, i] = parcel(r, slot_of(r, mate_h, i)).astype(BF16)

        swaps[r] = remote(
            mate_out.at[r], mate_parcel.at[r], parcel_send.at[r], parcel_recv.at[r], to_mate
        )
        swaps[r].start()

    def paired(r, i):
        return parcel(r, slot_of(r, h, i)) + mate_parcel[r, i].astype(F32)

    def send_back(r):
        swaps[r].wait()

        @pl.loop(0, half)
        def _(i):
            parcel_out[r, i] = paired(r, i).astype(BF16)

        backs[r] = remote(
            parcel_out.at[r], returned.at[r], back_send.at[r], back_recv.at[r], to_node[r]
        )
        backs[r].start()

    swap_with_mate(far)
    if far > 0:
        swap_with_mate(far - 1)
    swaps[far].wait()

    @pl.loop(0, quarter)
    def _(i):
        at = (opp // 2) * quarter + i
        parcel_out[far, quarter + i] = paired(far, at).astype(BF16)

    far_swap = remote(
        parcel_out.at[far, pl.ds(quarter, quarter)],
        far_in,
        far_send.at[0],
        far_recv.at[0],
        to_opp,
    )
    far_swap.start()
    if far > 0:
        send_back(far - 1)
    for r in order[2:]:
        swap_with_mate(r)
        send_back(r)

    cross.wait()
    theirs = part_feats.at[pl.ds(opp * own, own)]
    relay = remote(theirs, theirs, feat_send.at[2], feat_recv.at[2], to_mate)
    relay.start()
    far_swap.wait()

    @pl.loop(0, quarter)
    def _(i):
        total = paired(far, (f // 2) * quarter + i) + far_in[i].astype(F32)
        parcel_out[far, i] = total.astype(BF16)

    backs[far] = remote(
        parcel_out.at[far, pl.ds(0, quarter)],
        returned.at[far, pl.ds(0, quarter)],
        back_send.at[far],
        back_recv.at[far],
        to_node[far],
    )
    backs[far].start()
    pair.wait()
    relay.wait()
    outs = [None] * rounds
    my_quarter = arrived[far].at[pl.ds(f * quarter, quarter)]

    @pl.loop(0, quarter)
    def _(i):
        send_buf[far, i] = part_feats[meta[lay.send + far * need + f * quarter + i]]

    outs[far] = remote(
        send_buf.at[far, pl.ds(0, quarter)],
        my_quarter,
        node_send.at[far],
        node_recv.at[far],
        to_node[far],
    )
    outs[far].start()
    for r in order[1:]:

        @pl.loop(0, half)
        def _(i):
            send_buf[r, i] = part_feats[meta[lay.send + r * need + h * half + i]]

        outs[r] = remote(
            send_buf.at[r],
            arrived[r].at[pl.ds(h * half, half)],
            node_send.at[r],
            node_recv.at[r],
            to_node[r],
        )
        outs[r].start()

    def local_back(ts):
        prods = [dot_tn(local_values[0, 0, t], grad_hidden[meta[lay.rows + t]]) for t in ts]
        chain(sums_l, 0, ts, prods, lay.prev_l)

    grouped(lay.slots, local_back)

    def local_forward(ts):
        prods = [dot(local_values[0, 0, t], part_feats[meta[lay.cols + t]]) for t in ts]
        chain(sums_f, 0, ts, prods, lay.prev_f)

    grouped(lay.slots, local_forward)

    for r in order[::-1]:
        backs[r].wait()

    def gathered_sum(b):
        total = picked(sums_l, plan[lay.last_l + b])
        for r in range(rounds):
            count, first = (quarter, f * quarter) if r == far else (half, h * half)
            at = plan[lay.place + r * lay.part + b] - first
            there = jnp.logical_and(at >= 0, at < count)
            found = returned[r, jnp.clip(at, 0, count - 1)].astype(F32)
            total = total + jnp.where(there, found, 0.0)
        return total

    for o in range(feat_size // 2):

        @pl.loop(0, own)
        def _(j):
            pair_out[o, j] = gathered_sum((2 * o + mate_h) * own + j).astype(BF16)

    pair_red = remote(pair_out, pair_in, red_send.at[0], red_recv.at[0], to_mate)
    pair_red.start()
    for o in range(feat_size // 2):

        @pl.loop(0, own)
        def _(j):
            kept[o, j] = gathered_sum((2 * o + h) * own + j)

    pair_red.wait()

    @pl.loop(0, own)
    def _(j):
        o = opp // 2
        cross_out[j] = (kept[o, j] + pair_in[o, j].astype(F32)).astype(BF16)

    cross_red = remote(cross_out, cross_in, red_send.at[1], red_recv.at[1], to_opp)
    cross_red.start()
    passes = [None] * rounds

    def pass_on(r):
        outs[r].wait()
        piece = arrived[r].at[pl.ds(h * half, half)]
        passes[r] = remote(piece, piece, pass_send.at[r], pass_recv.at[r], to_mate)
        passes[r].start()

    def forward_products(r):
        if r < far:
            passes[r].wait()

        def step(ts):
            prods = [
                dot(
                    remote_values[0, 0, r, t],
                    arrived[r][meta[lay.rslots + r * lay.cap + t]],
                )
                for t in ts
            ]
            base = lay.slots + r * lay.cap
            chain(sums_f, base, ts, prods, lay.prev_f + base)

        grouped(lay.cap, step)

    def finish_grad():
        cross_red.wait()
        for j in range(own):
            o = f // 2
            total = kept[o, j] + pair_in[o, j].astype(F32)
            total = total + cross_in[j].astype(F32) + grad_hidden[j].astype(F32)
            grad_features[pl.ds(j * block, block), :] = total.astype(BF16)

    outs[far].wait()
    far_opp = remote(my_quarter, my_quarter, far_send.at[1], far_recv.at[1], to_opp)
    far_opp.start()
    far_mate = remote(my_quarter, my_quarter, pass_send.at[far], pass_recv.at[far], to_mate)
    far_mate.start()
    for r in range(far):
        pass_on(r)
        if r:
            forward_products(r - 1)
    finish_grad()
    far_opp.wait()
    opp_quarter = arrived[far].at[pl.ds(opp * quarter, quarter)]
    far_relay = remote(opp_quarter, opp_quarter, far_send.at[2], far_recv.at[2], to_mate)
    far_relay.start()
    if far > 0:
        forward_products(far - 1)
    far_mate.wait()
    far_relay.wait()
    forward_products(far)
    for d in range(own):
        rows = pl.ds(d * block, block)
        total = features[rows, :].astype(F32) + picked(sums_f, plan[lay.last_f + d])
        wide = jnp.concatenate([degree[d]] * (feat // block), axis=1)
        hidden = (total / wide).astype(BF16)
        output[rows, :] = dot(hidden, weight[...]).astype(BF16)


def body(
    features,
    weight,
    grad_out,
    local_rows,
    local_cols,
    local_values,
    remote_rows,
    remote_slots,
    remote_values,
    send_blocks,
    tile_counts,
):
    rows_dev, feat = features.shape
    block = local_values.shape[-1]
    own = rows_dev // block
    rounds, need = send_blocks.shape[1:]
    feat_size = lax.axis_size("feat")
    part = own * feat_size
    log_nodes = lax.axis_size("node").bit_length() - 1
    bits = [r * log_nodes // rounds for r in range(rounds)]
    half = need // 2
    assert feat_size == 4
    vmem = pl.BlockSpec(memory_space=pltpu.VMEM)
    smem = pl.BlockSpec(memory_space=pltpu.SMEM)
    slots, cap = local_values.shape[2], remote_values.shape[3]
    lay = Layout(slots, rounds, cap, need, own, part)
    tile_flops = 2 * block * block * feat * lay.tiles
    ints = (local_rows, local_cols, remote_rows, remote_slots, send_blocks, tile_counts)
    meta = jnp.concatenate([a.reshape(-1) for a in ints])
    plan, grad_hidden, degree = pl.pallas_call(
        functools.partial(plan_kernel, lay),
        out_shape=(
            jax.ShapeDtypeStruct((lay.plan_size,), jnp.int32),
            jax.ShapeDtypeStruct((own, block, feat), BF16),
            jax.ShapeDtypeStruct((own, block, block), F32),
        ),
        in_specs=[smem, vmem, vmem, vmem, vmem],
        out_specs=(smem, vmem, vmem),
        scratch_shapes=[pltpu.VMEM((own + 1, block, block), F32)],
        compiler_params=pltpu.CompilerParams(vmem_limit_bytes=VMEM_LIMIT),
        cost_estimate=pl.CostEstimate(
            flops=tile_flops // 2, bytes_accessed=4 * 2**20, transcendentals=0
        ),
        name="plan",
    )(meta, grad_out, weight, local_values, remote_values)
    dma = pltpu.SemaphoreType.DMA
    halves = pltpu.VMEM((rounds, half, block, feat), BF16)
    pairs = (feat_size // 2, own, block, feat)
    output, grad_features = pl.pallas_call(
        functools.partial(exchange_kernel, lay, bits, feat_size),
        out_shape=(
            jax.ShapeDtypeStruct((rows_dev, feat), BF16),
            jax.ShapeDtypeStruct((rows_dev, feat), BF16),
        ),
        in_specs=[smem, smem, vmem, vmem, vmem, vmem, vmem, vmem],
        out_specs=(vmem, vmem),
        scratch_shapes=[
            pltpu.VMEM((part, block, feat), BF16),
            halves,
            halves,
            halves,
            halves,
            halves,
            pltpu.VMEM(pairs, BF16),
            pltpu.VMEM(pairs, BF16),
            pltpu.VMEM(pairs, F32),
            pltpu.VMEM((own, block, feat), BF16),
            pltpu.VMEM((own, block, feat), BF16),
            pltpu.VMEM((rounds * cap, block, feat), F32),
            pltpu.VMEM((slots, block, feat), F32),
            pltpu.VMEM((lay.tiles, block, feat), F32),
            dma((3,)),
            dma((3,)),
            *[dma((rounds,))] * 8,
            dma((2,)),
            dma((2,)),
            dma((3,)),
            dma((3,)),
            pltpu.VMEM((half // 2, block, feat), BF16),
            *[pltpu.VMEM((need, block, feat), BF16)] * rounds,
        ],
        compiler_params=pltpu.CompilerParams(
            vmem_limit_bytes=VMEM_LIMIT, collective_id=0, has_side_effects=True
        ),
        cost_estimate=pl.CostEstimate(
            flops=2 * tile_flops, bytes_accessed=8 * 2**20, transcendentals=0
        ),
        name="exchange",
    )(meta, plan, features, weight, local_values, remote_values, grad_hidden, degree)
    return (output, grad_features)


def solution(mesh):
    in_specs = (
        P(("node", "feat"), None),
        P(),
        P(("node", "feat"), None),
        P("node", "feat", None),
        P("node", "feat", None),
        P("node", "feat", None, None, None),
        P("node", "feat", None, None),
        P("node", "feat", None, None),
        P("node", "feat", None, None, None, None),
        P("node", None, None),
        P("node", "feat", None),
    )
    out_specs = (P(("node", "feat"), None), P(("node", "feat"), None))
    return jax.shard_map(body, mesh=mesh, in_specs=in_specs, out_specs=out_specs, check_vma=False)
```

```python
import functools

import jax
import jax.numpy as jnp
from jax import lax
from jax.experimental import pallas as pl
from jax.experimental.pallas import tpu as pltpu
from jax.sharding import PartitionSpec as P

F32 = jnp.float32
BF16 = jnp.bfloat16
VMEM_LIMIT = 56 * 2**20
GROUP = 8


def dot(a, b):
    return jnp.dot(a, b, preferred_element_type=F32)


def dot_tn(a, b):
    return lax.dot_general(a, b, (((0,), (0,)), ((), ())), preferred_element_type=F32)


def dot_nt(a, b):
    return lax.dot_general(a, b, (((1,), (1,)), ((), ())), preferred_element_type=F32)


def grouped(slots, step):
    group = min(GROUP, slots)
    assert slots % group == 0

    @pl.loop(0, slots // group)
    def _(g):
        step([g * group + u for u in range(group)])


class Layout:
    def __init__(self, slots, rounds, cap, need, own, part):
        self.slots, self.rounds, self.cap, self.need = slots, rounds, cap, need
        self.own, self.part = own, part
        sizes = (slots, slots, rounds * cap, rounds * cap, rounds * need, rounds + 1)
        starts = [sum(sizes[:i]) for i in range(len(sizes) + 1)]
        self.rows, self.cols, self.rrows, self.rslots, self.send, self.counts, _ = starts
        tiles = slots + rounds * cap
        sizes = (tiles, own, slots, part, rounds * cap, rounds * need, rounds * part)
        starts = [sum(sizes[:i]) for i in range(len(sizes) + 1)]
        self.prev_f, self.last_f, self.prev_l, self.last_l = starts[:4]
        self.prev_r, self.last_r, self.place, self.plan_size = starts[4:]
        self.tiles = tiles


def plan_kernel(
    lay, meta, grad_out, weight, local_values, remote_values, plan, grad_hidden, degree, degree_sum
):
    block = local_values.shape[-1]
    feat = grad_out.shape[1]

    @pl.loop(0, lay.plan_size // GROUP)
    def _(i):
        for u in range(GROUP):
            plan[i * GROUP + u] = -1

    for i in range(lay.plan_size // GROUP * GROUP, lay.plan_size):
        plan[i] = -1

    @pl.loop(0, lay.slots)
    def _(t):
        @pl.when(t < meta[lay.counts])
        def _():
            d, c = meta[lay.rows + t], meta[lay.cols + t]
            plan[lay.prev_f + t] = plan[lay.last_f + d]
            plan[lay.last_f + d] = t
            plan[lay.prev_l + t] = plan[lay.last_l + c]
            plan[lay.last_l + c] = t

    for r in range(lay.rounds):

        @pl.loop(0, lay.cap)
        def _(t):
            at = r * lay.cap + t

            @pl.when(t < meta[lay.counts + r + 1])
            def _():
                d, c = meta[lay.rrows + at], meta[lay.rslots + at]
                plan[lay.prev_f + lay.slots + at] = plan[lay.last_f + d]
                plan[lay.last_f + d] = lay.slots + at
                plan[lay.prev_r + at] = plan[lay.last_r + r * lay.need + c]
                plan[lay.last_r + r * lay.need + c] = at

        @pl.loop(0, lay.need)
        def _(i):
            plan[lay.place + r * lay.part + meta[lay.send + r * lay.need + i]] = i

    ones = jnp.ones((block, block), BF16)
    degree_sum[...] = jnp.ones_like(degree_sum)

    def local_degree(ts):
        sums = [dot(local_values[0, 0, t], ones) for t in ts]
        for t, s in zip(ts, sums):
            to = jnp.where(t < meta[lay.counts], meta[lay.rows + t], lay.own)
            degree_sum[to] += s

    grouped(lay.slots, local_degree)
    for r in range(lay.rounds):

        def remote_degree(ts):
            sums = [dot(remote_values[0, 0, r, t], ones) for t in ts]
            for t, s in zip(ts, sums):
                live = t < meta[lay.counts + r + 1]
                to = jnp.where(live, meta[lay.rrows + r * lay.cap + t], lay.own)
                degree_sum[to] += s

        grouped(lay.cap, remote_degree)

    for d in range(lay.own):
        deg = degree_sum[d]
        degree[d] = deg
        dense = dot_nt(grad_out[pl.ds(d * block, block), :], weight[...])
        wide = jnp.concatenate([deg] * (feat // block), axis=1)
        grad_hidden[d] = (dense / wide).astype(BF16)


def exchange_kernel(
    lay,
    bits,
    feat_size,
    meta,
    plan,
    features,
    local_values,
    remote_values,
    grad_hidden,
    degree,
    hidden,
    grad_features,
    part_feats,
    send_buf,
    mate_out,
    mate_parcel,
    parcel_out,
    returned,
    pair_out,
    pair_in,
    kept,
    cross_out,
    cross_in,
    sums_r,
    sums_l,
    sums_f,
    feat_send,
    feat_recv,
    node_send,
    node_recv,
    pass_send,
    pass_recv,
    parcel_send,
    parcel_recv,
    back_send,
    back_recv,
    red_send,
    red_recv,
    *arrived,
):
    rounds = len(bits)
    own, block, feat = grad_hidden.shape
    need, half = lay.need, lay.need // 2
    node, f = lax.axis_index("node"), lax.axis_index("feat")
    h = lax.rem(f, 2)
    mate_h = 1 - h
    mate = f + 1 - 2 * h
    opp = lax.rem(f + 2, feat_size)
    partners = [node + (1 << b) * (1 - 2 * lax.rem(node // (1 << b), 2)) for b in bits]
    to_mate, to_opp = (node, mate), (node, opp)
    to_node = [(p, f) for p in partners]

    def remote(src, dst, send_sem, recv_sem, to):
        return pltpu.make_async_remote_copy(
            src_ref=src,
            dst_ref=dst,
            send_sem=send_sem,
            recv_sem=recv_sem,
            device_id=to,
            device_id_type=pl.DeviceIdType.MESH,
        )

    barrier = pltpu.get_barrier_semaphore()
    for to in (to_mate, to_opp, *to_node):
        pl.semaphore_signal(barrier, inc=1, device_id=to, device_id_type=pl.DeviceIdType.MESH)
    pl.semaphore_wait(barrier, 2 + rounds)

    mine = part_feats.at[pl.ds(f * own, own)]
    for b in range(own):
        part_feats[f * own + b] = features[pl.ds(b * block, block), :]
    cross = remote(mine, mine, feat_send.at[0], feat_recv.at[0], to_opp)
    cross.start()
    pair = remote(mine, mine, feat_send.at[1], feat_recv.at[1], to_mate)
    pair.start()
    order = list(range(rounds))[::-1]

    def picked(sums, at):
        return jnp.where(at >= 0, sums[jnp.maximum(at, 0)], 0.0)

    def chain(sums, base, ts, prods, prev):
        for t, p in zip(ts, prods):
            sums[base + t] = p + picked(sums, plan[prev + t])

    def back_products(r):
        def step(ts):
            prods = [
                dot_tn(remote_values[0, 0, r, t], grad_hidden[meta[lay.rrows + r * lay.cap + t]])
                for t in ts
            ]
            chain(sums_r, r * lay.cap, ts, prods, lay.prev_r + r * lay.cap)

        grouped(lay.cap, step)

    def parcel(r, s):
        return picked(sums_r, plan[lay.last_r + r * need + s])

    swaps, backs = [None] * rounds, [None] * rounds

    def send_back(r):
        swaps[r].wait()

        @pl.loop(0, half)
        def _(i):
            total = parcel(r, h * half + i) + mate_parcel[r, i].astype(F32)
            parcel_out[r, i] = total.astype(BF16)

        backs[r] = remote(
            parcel_out.at[r], returned.at[r], back_send.at[r], back_recv.at[r], to_node[r]
        )
        backs[r].start()

    for k, r in enumerate(order):
        back_products(r)

        @pl.loop(0, half)
        def _(i):
            mate_out[r, i] = parcel(r, mate_h * half + i).astype(BF16)

        swaps[r] = remote(
            mate_out.at[r], mate_parcel.at[r], parcel_send.at[r], parcel_recv.at[r], to_mate
        )
        swaps[r].start()
        if k:
            send_back(order[k - 1])
    send_back(order[-1])

    cross.wait()
    theirs = part_feats.at[pl.ds(opp * own, own)]
    relay = remote(theirs, theirs, feat_send.at[2], feat_recv.at[2], to_mate)
    relay.start()
    pair.wait()
    relay.wait()
    outs = [None] * rounds
    for r in order:

        @pl.loop(0, half)
        def _(i):
            send_buf[r, i] = part_feats[meta[lay.send + r * need + h * half + i]]

        outs[r] = remote(
            send_buf.at[r],
            arrived[r].at[pl.ds(h * half, half)],
            node_send.at[r],
            node_recv.at[r],
            to_node[r],
        )
        outs[r].start()

    def local_back(ts):
        prods = [dot_tn(local_values[0, 0, t], grad_hidden[meta[lay.rows + t]]) for t in ts]
        chain(sums_l, 0, ts, prods, lay.prev_l)

    grouped(lay.slots, local_back)

    def local_forward(ts):
        prods = [dot(local_values[0, 0, t], part_feats[meta[lay.cols + t]]) for t in ts]
        chain(sums_f, 0, ts, prods, lay.prev_f)

    grouped(lay.slots, local_forward)

    for r in order[::-1]:
        backs[r].wait()

    def gathered_sum(b):
        total = picked(sums_l, plan[lay.last_l + b])
        for r in range(rounds):
            at = plan[lay.place + r * lay.part + b] - h * half
            there = jnp.logical_and(at >= 0, at < half)
            found = returned[r, jnp.clip(at, 0, half - 1)].astype(F32)
            total = total + jnp.where(there, found, 0.0)
        return total

    for o in range(feat_size // 2):

        @pl.loop(0, own)
        def _(j):
            pair_out[o, j] = gathered_sum((2 * o + mate_h) * own + j).astype(BF16)

    pair_red = remote(pair_out, pair_in, red_send.at[0], red_recv.at[0], to_mate)
    pair_red.start()
    for o in range(feat_size // 2):

        @pl.loop(0, own)
        def _(j):
            kept[o, j] = gathered_sum((2 * o + h) * own + j)

    pair_red.wait()

    @pl.loop(0, own)
    def _(j):
        o = opp // 2
        cross_out[j] = (kept[o, j] + pair_in[o, j].astype(F32)).astype(BF16)

    cross_red = remote(cross_out, cross_in, red_send.at[1], red_recv.at[1], to_opp)
    cross_red.start()
    passes = [None] * rounds

    def pass_on(r):
        outs[r].wait()
        piece = arrived[r].at[pl.ds(h * half, half)]
        passes[r] = remote(piece, piece, pass_send.at[r], pass_recv.at[r], to_mate)
        passes[r].start()

    def forward_products(r):
        passes[r].wait()

        def step(ts):
            prods = [
                dot(
                    remote_values[0, 0, r, t],
                    arrived[r][meta[lay.rslots + r * lay.cap + t]],
                )
                for t in ts
            ]
            base = lay.slots + r * lay.cap
            chain(sums_f, base, ts, prods, lay.prev_f + base)

        grouped(lay.cap, step)

    for r in range(rounds):
        pass_on(r)
        if r:
            forward_products(r - 1)
        if r == rounds - 2:
            cross_red.wait()
            for j in range(own):
                o = f // 2
                total = kept[o, j] + pair_in[o, j].astype(F32)
                total = total + cross_in[j].astype(F32) + grad_hidden[j].astype(F32)
                grad_features[pl.ds(j * block, block), :] = total.astype(BF16)
    forward_products(rounds - 1)
    for d in range(own):
        rows = pl.ds(d * block, block)
        total = features[rows, :].astype(F32) + picked(sums_f, plan[lay.last_f + d])
        wide = jnp.concatenate([degree[d]] * (feat // block), axis=1)
        hidden[rows, :] = (total / wide).astype(BF16)


def body(
    features,
    weight,
    grad_out,
    local_rows,
    local_cols,
    local_values,
    remote_rows,
    remote_slots,
    remote_values,
    send_blocks,
    tile_counts,
):
    rows_dev, feat = features.shape
    block = local_values.shape[-1]
    own = rows_dev // block
    rounds, need = send_blocks.shape[1:]
    feat_size = lax.axis_size("feat")
    part = own * feat_size
    log_nodes = lax.axis_size("node").bit_length() - 1
    bits = [r * log_nodes // rounds for r in range(rounds)]
    half = need // 2
    assert feat_size == 4
    vmem = pl.BlockSpec(memory_space=pltpu.VMEM)
    smem = pl.BlockSpec(memory_space=pltpu.SMEM)
    slots, cap = local_values.shape[2], remote_values.shape[3]
    lay = Layout(slots, rounds, cap, need, own, part)
    tile_flops = 2 * block * block * feat * lay.tiles
    ints = (local_rows, local_cols, remote_rows, remote_slots, send_blocks, tile_counts)
    meta = jnp.concatenate([a.reshape(-1) for a in ints])
    plan, grad_hidden, degree = pl.pallas_call(
        functools.partial(plan_kernel, lay),
        out_shape=(
            jax.ShapeDtypeStruct((lay.plan_size,), jnp.int32),
            jax.ShapeDtypeStruct((own, block, feat), BF16),
            jax.ShapeDtypeStruct((own, block, block), F32),
        ),
        in_specs=[smem, vmem, vmem, vmem, vmem],
        out_specs=(smem, vmem, vmem),
        scratch_shapes=[pltpu.VMEM((own + 1, block, block), F32)],
        compiler_params=pltpu.CompilerParams(vmem_limit_bytes=VMEM_LIMIT),
        cost_estimate=pl.CostEstimate(
            flops=tile_flops // 2, bytes_accessed=4 * 2**20, transcendentals=0
        ),
        name="plan",
    )(meta, grad_out, weight, local_values, remote_values)
    dma = pltpu.SemaphoreType.DMA
    halves = pltpu.VMEM((rounds, half, block, feat), BF16)
    pairs = (feat_size // 2, own, block, feat)
    hidden, grad_features = pl.pallas_call(
        functools.partial(exchange_kernel, lay, bits, feat_size),
        out_shape=(
            jax.ShapeDtypeStruct((rows_dev, feat), BF16),
            jax.ShapeDtypeStruct((rows_dev, feat), BF16),
        ),
        in_specs=[smem, smem, vmem, vmem, vmem, vmem, vmem],
        out_specs=(vmem, vmem),
        scratch_shapes=[
            pltpu.VMEM((part, block, feat), BF16),
            halves,
            halves,
            halves,
            halves,
            halves,
            pltpu.VMEM(pairs, BF16),
            pltpu.VMEM(pairs, BF16),
            pltpu.VMEM(pairs, F32),
            pltpu.VMEM((own, block, feat), BF16),
            pltpu.VMEM((own, block, feat), BF16),
            pltpu.VMEM((rounds * cap, block, feat), F32),
            pltpu.VMEM((slots, block, feat), F32),
            pltpu.VMEM((lay.tiles, block, feat), F32),
            dma((3,)),
            dma((3,)),
            *[dma((rounds,))] * 8,
            dma((2,)),
            dma((2,)),
            *[pltpu.VMEM((need, block, feat), BF16)] * rounds,
        ],
        compiler_params=pltpu.CompilerParams(
            vmem_limit_bytes=VMEM_LIMIT, collective_id=0, has_side_effects=True
        ),
        cost_estimate=pl.CostEstimate(
            flops=2 * tile_flops, bytes_accessed=8 * 2**20, transcendentals=0
        ),
        name="exchange",
    )(meta, plan, features, local_values, remote_values, grad_hidden, degree)
    output = dot(hidden, weight).astype(BF16)
    return (output, grad_features)


def solution(mesh):
    in_specs = (
        P(("node", "feat"), None),
        P(),
        P(("node", "feat"), None),
        P("node", "feat", None),
        P("node", "feat", None),
        P("node", "feat", None, None, None),
        P("node", "feat", None, None),
        P("node", "feat", None, None),
        P("node", "feat", None, None, None, None),
        P("node", None, None),
        P("node", "feat", None),
    )
    out_specs = (P(("node", "feat"), None), P(("node", "feat"), None))
    return jax.shard_map(body, mesh=mesh, in_specs=in_specs, out_specs=out_specs, check_vma=False)
```
